256 devices in a mesh: reader: 4 (over x), pixel: 8 (over y, core), blk: 8 (over z).
Axes of the slice: x: 4, y: 4, z: 8, core: 2. Of those that a mesh axis runs over, the one named last changes fastest.
Arguments:
- intensity: bfloat16 [640, 262144], P('reader', ('pixel', 'blk')), may hold values from 0.049804688 to 20
- labels: int32 [262144, 1], P(('pixel', 'blk')), may hold values from 0 to 255; in each aligned block of 4096 rows (0 to 4095, 4096 to 8191, ...) at most 32 rows name the same one
Outputs:
- correlation: float32 [256, 640, 640], P(('reader', 'pixel', 'blk'))
The draws below stay inside these ranges and needn't reach their ends.
Inputs may be any that keep to these rules, and one draw needn't show every extreme that they name: `labels`: among the pixels of one device (each aligned block of 4096 pixels) no q-cycle has more than 32 pixels, and some q-cycle has exactly 32; every q-cycle has at least one pixel.
All inputs are finite; a program needn't handle non-finite values.
Results may differ from the reference program's by a relative error of at most 0.0003.
Values may be sent and summed in bfloat16 or wider, within the bound.
No kernel may reach another device: no remote copies, remote signals or barrier semaphores. Data moves between devices by JAX's collectives and lax.ppermute only.
A program may use at most 64 MiB of HBM per device.

```python
import math
import jax
import jax.numpy as jnp
import numpy as np
from jax import lax

F = 640
CYCLES = 256
PIX_DEV = 4096
CAPR = 32
NPIX = 262144
N_PIXEL = 8
N_BLK = 8


def steps_of(own_key, extent, pieces, least, high):
    def one(axis_at, parts):
        draws = jax.random.uniform(jax.random.fold_in(jax.random.fold_in(own_key, 6), axis_at), (parts,), jnp.float32, least / len(pieces), high / len(pieces))
        return jnp.repeat(jnp.exp(draws), extent[axis_at] // parts).reshape((-1,) + (1,) * (len(extent) - axis_at - 1))

    loudness = one(*pieces[0])
    for cut in pieces[1:]:
        loudness = loudness * one(*cut)
    return loudness


def routed_block(own_key, own, number, rows, amount, top, bound, slope):
    sequence = jax.random.permutation(own_key, amount)
    heavy_load, usual = portions_of(amount, rows * top, bound, slope, True), portions_of(amount, rows * top, bound, slope, False)
    places = jnp.arange(amount)

    def named(tallies, turn):
        used = int((tallies > 0).sum())
        fixed = max(1, used // 4)
        moved = fixed + (places - fixed + turn * (used - fixed)) % max(1, amount - fixed)
        return jnp.zeros((amount,), jnp.int32).at[sequence[jnp.where(places < fixed, places, moved)]].set(jnp.asarray(tallies, jnp.int32))

    tallies = jnp.where(number % 4 == 0, named(heavy_load, number // 4), named(usual, number - number // 4 - 1))
    mixed = jax.random.permutation(jax.random.fold_in(own, 3), amount)
    source_of, receiver = mixed[0:amount // 2 * 2:2], mixed[1:amount // 2 * 2:2]
    room = jnp.minimum(tallies[source_of] - 1, bound - tallies[receiver]) // 2
    room = jnp.where((source_of == sequence[0]) | (receiver == sequence[0]) | (tallies[receiver] == 0), 0, jnp.maximum(room, 0))
    moved = jax.random.randint(jax.random.fold_in(own, 4), (amount // 2,), 0, 1 << 20) % (room + 1)
    tallies = tallies.at[source_of].add(-moved).at[receiver].add(moved)
    members = jnp.searchsorted(jnp.cumsum(tallies), jnp.arange(rows * top), side="right").astype(jnp.int32)
    grid = members.reshape(top, rows).T
    grid = grid[jax.random.permutation(jax.random.fold_in(own, 1), rows)]
    turn = jax.random.randint(jax.random.fold_in(own, 2), (rows, 1), 0, top)
    return jnp.take_along_axis(grid, (jnp.arange(top)[None, :] + turn) % top, axis=1)


def portions_of(number_of, total, limit, skew, full):
    loads = [(1 << 20) // math.isqrt(rank ** skew) + 1 for rank in range(1, number_of + 1)]
    largest = limit if full else min(limit, max(-(-total // number_of), total * loads[0] // sum(loads)))
    least = 1 if total - largest >= number_of - 1 else 0
    holding, spare = [largest] + [least] * (number_of - 1), total - largest - least * (number_of - 1)
    while spare > 0:
        free = [i for i in range(1, number_of) if holding[i] < largest] or [i for i in range(1, number_of) if holding[i] < limit]
        pool, budget = sum([loads[i] for i in free]), spare
        for i in free:
            more = min(limit - holding[i], max(1, budget * loads[i] // pool), spare)
            holding[i] = holding[i] + more
            spare = spare - more
    return np.array(holding)


def setup_inputs(seed: int = 0) -> dict:
    key_list = jax.random.split(jax.random.key(seed), 3)
    intensity = jnp.clip(jnp.exp(math.log(20.0) - 5.9953784 * jax.random.uniform(key_list[0], (F, NPIX), jnp.float32) ** steps_of(key_list[0], (F, NPIX), ((0, 4), (1, 64)), -0.2, 0.2)), 0.049804688, 20.0).astype(jnp.bfloat16)
    labels_keys = jax.random.split(jax.random.fold_in(key_list[1], 1), NPIX // PIX_DEV)
    labels_turns = jax.random.permutation(jax.random.fold_in(key_list[1], 3), NPIX // PIX_DEV)
    labels = jax.vmap(lambda own, number: routed_block(jax.random.fold_in(key_list[1], 2), own, number, PIX_DEV, CYCLES, 1, CAPR, 2))(labels_keys, labels_turns).reshape((NPIX, 1))
    return {"intensity": intensity, "labels": labels}


def reference(intensity, labels):
    lab = labels[:, 0].astype(jnp.int32)
    total = lab.shape[0]
    order = jnp.argsort(lab, stable=True).astype(jnp.int32)
    sorted_lab = lab[order]
    cycle_ids = jnp.arange(CYCLES, dtype=jnp.int32)
    starts = jnp.searchsorted(sorted_lab, cycle_ids, side="left").astype(jnp.int32)
    counts = jnp.searchsorted(sorted_lab, cycle_ids, side="right").astype(jnp.int32) - starts
    span = N_PIXEL * N_BLK * CAPR
    offsets = jnp.arange(span, dtype=jnp.int32)

    def one_cycle(cycle):
        start = starts[cycle]
        count = counts[cycle]
        pixels = order[jnp.minimum(start + offsets, total - 1)]
        block = jnp.take(intensity, pixels, axis=1)
        block = jnp.where((offsets < count)[None, :], block, jnp.zeros((), intensity.dtype))
        gram = jnp.dot(block, block.T, preferred_element_type=jnp.float32)
        cycle_sum = jnp.sum(block.astype(jnp.float32), axis=1)
        return count.astype(jnp.float32) * gram / (cycle_sum[:, None] * cycle_sum[None, :])

    return lax.map(one_cycle, cycle_ids)
```

```python
import functools

import jax
import jax.numpy as jnp
from jax import lax
from jax.experimental import pallas as pl
from jax.experimental.pallas import tpu as pltpu
from jax.sharding import PartitionSpec as P

CYCLES = 256
CAPR = 32
AXES = ("reader", "pixel", "blk")
LANES = 128
WIDE = 256
PACK = LANES // CAPR


def swap_blocks(tile):
    height = tile.shape[0] // PACK
    block_of = lax.broadcasted_iota(jnp.int32, (height, LANES), 1) // CAPR
    turned = []
    for a in range(PACK):
        part = tile[a * height:(a + 1) * height]
        turned.append(pltpu.roll(part, CAPR * a, 1) if a else part)
    out = []
    for b in range(PACK):
        merged = turned[(0 - b) % PACK]
        for j in range(1, PACK):
            merged = jnp.where(block_of == j, turned[(j - b) % PACK], merged)
        out.append(pltpu.roll(merged, LANES - CAPR * b, 1) if b else merged)
    return jnp.concatenate(out, axis=0)


def pick_kernel(lab_ref, x_ref, out_ref, low_ref, high_ref):
    pixels = x_ref.shape[1]
    step = pl.program_id(0)

    @pl.when(step == 0)
    def _():
        row = lax.broadcasted_iota(jnp.int32, (WIDE, WIDE), 0)
        col = lax.broadcasted_iota(jnp.int32, (WIDE, WIDE), 1)
        before = (col < row).astype(jnp.bfloat16)
        ones = jnp.ones((WIDE, WIDE), jnp.bfloat16)
        carry = jnp.zeros((1, CYCLES), jnp.float32)
        for i in range(pixels // WIDE):
            lab_row = lab_ref[i:i + 1, :].astype(jnp.float32)
            spread = jnp.where(row == col, lab_row, 0.0).astype(jnp.bfloat16)
            lab = jnp.dot(spread, ones, preferred_element_type=jnp.float32)
            member = (lab == col.astype(jnp.float32)).astype(jnp.float32)
            member16 = member.astype(jnp.bfloat16)
            earlier = jnp.dot(before, member16, preferred_element_type=jnp.float32) + carry
            carry = earlier[WIDE - 1:] + member[WIDE - 1:]
            rank = jnp.dot((member * earlier).astype(jnp.bfloat16), ones[:, :LANES], preferred_element_type=jnp.float32)
            slot = lab[:, :LANES].astype(jnp.int32) * CAPR + rank.astype(jnp.int32)
            low_ref[i * WIDE:(i + 1) * WIDE, :] = (slot & (WIDE - 1)).astype(jnp.bfloat16)
            high_ref[i * WIDE:(i + 1) * WIDE, :] = (slot >> 8).astype(jnp.bfloat16)

    lane = lax.broadcasted_iota(jnp.int32, (pixels, LANES), 1).astype(jnp.bfloat16)
    here = jnp.where(high_ref[...] == step.astype(jnp.bfloat16), low_ref[...], jnp.bfloat16(-1))
    one, zero = jnp.bfloat16(1), jnp.bfloat16(0)
    chosen = jnp.concatenate(
        [jnp.where(here == lane + jnp.bfloat16(h * LANES), one, zero) for h in range(WIDE // LANES)], axis=1
    )
    picked = jnp.dot(x_ref[...], chosen, preferred_element_type=jnp.float32)
    rows = x_ref.shape[0]
    for h in range(WIDE // LANES):
        out_ref[h * rows:(h + 1) * rows, :] = swap_blocks(picked[:, h * LANES:(h + 1) * LANES]).astype(jnp.bfloat16)


def pick(intensity, labels):
    frames, pixels = intensity.shape
    slots = CYCLES * CAPR
    steps = slots // WIDE
    return pl.pallas_call(
        pick_kernel,
        grid=(steps,),
        in_specs=[
            pl.BlockSpec((pixels // WIDE, WIDE), lambda i: (0, 0)),
            pl.BlockSpec((frames, pixels), lambda i: (0, 0)),
        ],
        out_specs=pl.BlockSpec((frames * WIDE // LANES, LANES), lambda i: (i, 0)),
        out_shape=jax.ShapeDtypeStruct((frames * slots // LANES, LANES), jnp.bfloat16),
        scratch_shapes=[pltpu.VMEM((pixels, LANES), jnp.bfloat16), pltpu.VMEM((pixels, LANES), jnp.bfloat16)],
        compiler_params=pltpu.CompilerParams(vmem_limit_bytes=48 * 2**20),
        name="pick_pixels",
    )(labels.reshape(pixels // WIDE, WIDE), intensity)


def gram_kernel(per, got_ref, out_ref, all_ref):
    total, slots = all_ref.shape
    groups = slots // LANES
    for r in range(total // per):
        for g in range(groups):
            at = (r * groups + g) * per
            tile = swap_blocks(got_ref[at:at + per, :].astype(jnp.float32))
            all_ref[r * per:(r + 1) * per, g * LANES:(g + 1) * LANES] = tile.astype(jnp.bfloat16)
    series = all_ref[...]
    across = (((1,), (1,)), ((), ()))
    gram = lax.dot_general(series, series, across, preferred_element_type=jnp.float32)
    sum_col = jnp.dot(series, jnp.ones((slots, LANES), jnp.bfloat16), preferred_element_type=jnp.float32)
    sum_row = lax.dot_general(jnp.ones((8, slots), jnp.bfloat16), series, across, preferred_element_type=jnp.float32)
    count = jnp.sum((all_ref[0:16, :].astype(jnp.float32)[0:1] > 0).astype(jnp.float32), axis=1, keepdims=True)
    left = count / sum_col[:, :1]
    right = 1.0 / sum_row[:1]
    out_ref[0] = gram * left * right


def correlate(got, frames, total, slots):
    return pl.pallas_call(
        functools.partial(gram_kernel, frames),
        out_shape=jax.ShapeDtypeStruct((1, total, total), jnp.float32),
        in_specs=[pl.BlockSpec(memory_space=pltpu.VMEM)],
        out_specs=pl.BlockSpec(memory_space=pltpu.VMEM),
        scratch_shapes=[pltpu.VMEM((total, slots), jnp.bfloat16)],
        compiler_params=pltpu.CompilerParams(vmem_limit_bytes=48 * 2**20),
        name="correlate",
    )(got)


def body(intensity, labels):
    readers = lax.axis_size("reader")
    groups = lax.axis_size("pixel") * lax.axis_size("blk")
    outgoing = pick(intensity, labels)
    got = lax.all_to_all(outgoing, AXES, split_axis=0, concat_axis=0, tiled=True)
    return correlate(got, intensity.shape[0], intensity.shape[0] * readers, groups * CAPR)


def solution(mesh):
    placed = (P("reader", ("pixel", "blk")), P(("pixel", "blk"), None))
    return jax.shard_map(
        body,
        mesh=mesh,
        in_specs=placed,
        out_specs=P(AXES, None, None),
        check_vma=False,
    )
```

```python
import functools

import jax
import jax.numpy as jnp
from jax import lax
from jax.experimental import pallas as pl
from jax.experimental.pallas import tpu as pltpu
from jax.sharding import PartitionSpec as P

CYCLES = 256
CAPR = 32
AXES = ("reader", "pixel", "blk")
LANES = 128
WIDE = 256
PACK = LANES // CAPR
SHORT = CAPR // PACK
ROWS = CAPR + SHORT
PARTS = 4
CHUNKS = 8
NN = (((1,), (0,)), ((), ()))
NT = (((1,), (1,)), ((), ()))
TN = (((0,), (0,)), ((), ()))


def dot(a, b, dims=NN):
    return lax.dot_general(a, b, dims, preferred_element_type=jnp.float32)


def swap_blocks(tile):
    height = tile.shape[0] // PACK
    block_of = lax.broadcasted_iota(jnp.int32, (height, LANES), 1) // CAPR
    turned = []
    for a in range(PACK):
        part = tile[a * height:(a + 1) * height]
        turned.append(pltpu.roll(part, CAPR * a, 1) if a else part)
    out = []
    for b in range(PACK):
        merged = turned[(0 - b) % PACK]
        for j in range(1, PACK):
            merged = jnp.where(block_of == j, turned[(j - b) % PACK], merged)
        out.append(pltpu.roll(merged, LANES - CAPR * b, 1) if b else merged)
    return jnp.concatenate(out, axis=0)


def pick_kernel(turn_ref, lab_hbm, x_ref, out_ref, lab_ref, frames_ref, place_ref, table_ref, main_ref, rest_ref,
                send_ref, scalars, sems, small_sems, out_sems):
    pixels = x_ref.shape[1]
    part = pixels // PARTS
    turn = turn_ref[0]
    lab_copy = pltpu.make_async_copy(lab_hbm, lab_ref, small_sems.at[0])
    lab_copy.start()
    copies = []
    for b in range(PACK):
        to = pl.multiple_of(((b + turn) % PACK) * CAPR, CAPR)
        copies.append(pltpu.make_async_copy(x_ref.at[pl.ds(b * CAPR, CAPR)], frames_ref.at[pl.ds(to, CAPR)], sems.at[b]))
        copies.append(pltpu.make_async_copy(
            x_ref.at[pl.ds(LANES, CAPR)], frames_ref.at[pl.ds(LANES + b * CAPR, CAPR)], sems.at[PACK + b]))
    for copy in copies:
        copy.start()

    row = lax.broadcasted_iota(jnp.int32, (WIDE, WIDE), 0)
    col = lax.broadcasted_iota(jnp.int32, (WIDE, WIDE), 1)
    upper = (row < col).astype(jnp.bfloat16)
    lower = (col < row).astype(jnp.bfloat16)
    ones = jnp.ones((WIDE, LANES), jnp.bfloat16)
    blocks = part // WIDE
    lab_copy.wait()
    member = jnp.concatenate(
        [(lab_ref[:, i * WIDE:(i + 1) * WIDE] == row).astype(jnp.bfloat16) for i in range(pixels // WIDE)], axis=0)
    earlier = dot(member, upper)
    counts = dot(member, ones)
    done = jnp.zeros((CYCLES, LANES), jnp.float32)
    for h in range(PARTS):
        count = [counts[i * CYCLES:(i + 1) * CYCLES] for i in range(h * blocks, (h + 1) * blocks)]
        total = functools.reduce(lambda a, b: a + b, count)
        base = dot(lower, total.astype(jnp.bfloat16))
        table_ref[2 * h * 8:(2 * h + 1) * 8, :] = (base - done + CAPR).T[:8].astype(jnp.int32)
        done = done + total
        table_ref[(2 * h + 1) * 8:(2 * h + 2) * 8, :] = done.T[:8].astype(jnp.int32)
        for i in range(blocks):
            at = h * part + i * WIDE
            from_row = (h * blocks + i) * CYCLES
            spot = earlier[from_row:from_row + CYCLES] + jnp.concatenate([base, base], axis=1)
            place_ref[:, at:at + WIDE] = jnp.sum(
                jnp.where(lab_ref[:, at:at + WIDE] == row, spot, 0.0), axis=0, keepdims=True)
            base = base + count[i]
    table_copy = pltpu.make_async_copy(table_ref, scalars, small_sems.at[1])
    table_copy.start()

    for copy in copies:
        copy.wait()
    spot = lax.broadcasted_iota(jnp.int32, (part, part), 0).astype(jnp.float32)
    block_of = lax.broadcasted_iota(jnp.int32, (CAPR + part, LANES), 1) // CAPR
    for h in range(PARTS):
        chosen = (spot == place_ref[:, h * part:(h + 1) * part]).astype(jnp.bfloat16)
        ordered = dot(chosen, frames_ref[:, h * part:(h + 1) * part], NT)
        main_ref[h, CAPR:CAPR + part, :] = ordered[:, :LANES]
        tail = jnp.concatenate([jnp.zeros((CAPR, LANES), jnp.float32), ordered[:, LANES:]], axis=0)
        folded = tail
        for q in range(1, PACK):
            shifted = jnp.concatenate([tail[q * SHORT:], tail[:q * SHORT]], axis=0)
            folded = jnp.where(block_of == q, shifted, folded)
        rest_ref[h, :CAPR + part, :] = folded

    table_copy.wait()
    slot = lax.broadcasted_iota(jnp.int32, (CAPR, LANES), 0)
    slot_rest = lax.broadcasted_iota(jnp.int32, (SHORT, LANES), 0) + SHORT * block_of[:SHORT]

    def spread(pair, carry):
        parts = []
        for odd in range(2):
            cycle = pair * 2 + odd
            main = jnp.zeros((CAPR, LANES), jnp.float32)
            rest = jnp.zeros((SHORT, LANES), jnp.float32)
            for h in reversed(range(PARTS)):
                at = scalars[2 * h * 8, cycle]
                end = scalars[(2 * h + 1) * 8, cycle]
                main = jnp.where(slot < end, main_ref[h, pl.ds(at, CAPR), :], main)
                rest = jnp.where(slot_rest < end, rest_ref[h, pl.ds(at, SHORT), :], rest)
            parts += [main, rest]
        to = pl.multiple_of(pair * (2 * ROWS), 2 * ROWS)
        send_ref[pl.ds(to, 2 * ROWS), :] = jnp.concatenate(parts, axis=0).astype(jnp.bfloat16)
        return carry

    pairs = CYCLES // 2 // CHUNKS
    outs = []
    for c in range(CHUNKS):
        lax.fori_loop(c * pairs, (c + 1) * pairs, spread, 0, unroll=4)
        rows = pl.ds(c * pairs * 2 * ROWS, pairs * 2 * ROWS)
        outs.append(pltpu.make_async_copy(send_ref.at[rows], out_ref.at[rows], out_sems.at[c]))
        outs[-1].start()
    for copy in outs:
        copy.wait()


def pick(intensity, labels, turn):
    pixels = intensity.shape[1]
    part = pixels // PARTS
    return pl.pallas_call(
        pick_kernel,
        in_specs=[
            pl.BlockSpec(memory_space=pltpu.SMEM),
            pl.BlockSpec(memory_space=pl.ANY),
            pl.BlockSpec(memory_space=pl.ANY),
        ],
        out_specs=pl.BlockSpec(memory_space=pl.ANY),
        out_shape=jax.ShapeDtypeStruct((CYCLES * ROWS, LANES), jnp.bfloat16),
        scratch_shapes=[
            pltpu.VMEM((1, pixels), jnp.int32),
            pltpu.VMEM((2 * LANES, pixels), jnp.bfloat16),
            pltpu.VMEM((1, pixels), jnp.float32),
            pltpu.VMEM((2 * PARTS * 8, CYCLES), jnp.int32),
            pltpu.VMEM((PARTS, part + 2 * CAPR, LANES), jnp.float32),
            pltpu.VMEM((PARTS, part + 2 * CAPR, LANES), jnp.float32),
            pltpu.VMEM((CYCLES * ROWS, LANES), jnp.bfloat16),
            pltpu.SMEM((2 * PARTS * 8, CYCLES), jnp.int32),
            pltpu.SemaphoreType.DMA((2 * PACK,)),
            pltpu.SemaphoreType.DMA((2,)),
            pltpu.SemaphoreType.DMA((CHUNKS,)),
        ],
        compiler_params=pltpu.CompilerParams(vmem_limit_bytes=60 * 2**20),
        name="pick_pixels",
    )(turn, labels.reshape(1, pixels), intensity)


def gram_kernel(got_ref, out_ref, all_ref):
    groups = all_ref.shape[0] // CAPR
    block_of = lax.broadcasted_iota(jnp.int32, (CAPR, LANES), 1) // CAPR
    filled = jnp.zeros((CAPR, LANES), jnp.float32)
    for g in range(0, groups, 2):
        got = [got_ref[(r * groups + g) * ROWS:(r * groups + g + 2) * ROWS, :].astype(jnp.float32) for r in range(PACK)]
        both = []
        for odd in range(2):
            m = [x[odd * ROWS:odd * ROWS + CAPR] for x in got]
            rest = swap_blocks(jnp.concatenate([x[odd * ROWS + CAPR:(odd + 1) * ROWS] for x in got], axis=0))
            filled = filled + (m[0] > 0).astype(jnp.float32)
            tiles = []
            for t in range(PACK + 1):
                tile = rest
                if t > 0:
                    tile = jnp.where(block_of < t - 1, m[t - 1], tile)
                if t < PACK:
                    tile = jnp.where(block_of >= t, m[t], tile)
                tiles.append(tile)
            both.append(jnp.concatenate(tiles, axis=1))
        all_ref[g * CAPR:(g + 2) * CAPR, :] = jnp.concatenate(both, axis=0).astype(jnp.bfloat16)
    series = all_ref[...]
    gram = dot(series, series, TN)
    sums = dot(jnp.ones((8, series.shape[0]), jnp.bfloat16), series)
    count = jnp.sum(filled, axis=0, keepdims=True)[:, :1]
    out_ref[0] = gram * (count / sums.T[:, :1]) * (1.0 / sums[:1])


def correlate(got, total):
    slots = got.shape[0] * LANES // total
    return pl.pallas_call(
        gram_kernel,
        out_shape=jax.ShapeDtypeStruct((1, total, total), jnp.float32),
        in_specs=[pl.BlockSpec(memory_space=pltpu.VMEM)],
        out_specs=pl.BlockSpec(memory_space=pltpu.VMEM),
        scratch_shapes=[pltpu.VMEM((slots, total), jnp.bfloat16)],
        compiler_params=pltpu.CompilerParams(vmem_limit_bytes=48 * 2**20),
        name="correlate",
    )(got)


def body(intensity, labels):
    turn = lax.axis_index("reader").astype(jnp.int32).reshape(1)
    outgoing = pick(intensity, labels, turn)
    got = lax.all_to_all(outgoing, AXES, split_axis=0, concat_axis=0, tiled=True)
    return correlate(got, intensity.shape[0] * lax.axis_size("reader"))


def solution(mesh):
    placed = (P("reader", ("pixel", "blk")), P(("pixel", "blk"), None))
    return jax.shard_map(
        body,
        mesh=mesh,
        in_specs=placed,
        out_specs=P(AXES, None, None),
        check_vma=False,
    )
```

```python
import functools

import jax
import jax.numpy as jnp
from jax import lax
from jax.experimental import pallas as pl
from jax.experimental.pallas import tpu as pltpu
from jax.sharding import PartitionSpec as P

CYCLES = 256
CAPR = 32
AXES = ("reader", "pixel", "blk")
ROUTE = ("pixel", "reader", "blk")
LANES = 128
WIDE = 256
PACK = LANES // CAPR
SHORT = CAPR // PACK
ROWS = CAPR + SHORT
PARTS = 4
CHUNKS = 8
TALL = 128
NN = (((1,), (0,)), ((), ()))
NT = (((1,), (1,)), ((), ()))
TN = (((0,), (0,)), ((), ()))


def dot(a, b, dims=NN):
    return lax.dot_general(a, b, dims, preferred_element_type=jnp.float32)


def swap_blocks(tile):
    height = tile.shape[0] // PACK
    block_of = lax.broadcasted_iota(jnp.int32, (height, LANES), 1) // CAPR
    turned = []
    for a in range(PACK):
        part = tile[a * height:(a + 1) * height]
        turned.append(pltpu.roll(part, CAPR * a, 1) if a else part)
    out = []
    for b in range(PACK):
        merged = turned[(0 - b) % PACK]
        for j in range(1, PACK):
            merged = jnp.where(block_of == j, turned[(j - b) % PACK], merged)
        out.append(pltpu.roll(merged, LANES - CAPR * b, 1) if b else merged)
    return jnp.concatenate(out, axis=0)


def pick_kernel(readers, blks, turn_ref, lab_hbm, x_ref, out_ref, lab_ref, frames_ref, place_ref, table_ref, main_ref, rest_ref,
                send_ref, scalars, sems, small_sems, out_sems):
    pixels = x_ref.shape[1]
    part = pixels // PARTS
    turn = turn_ref[0]
    lab_copy = pltpu.make_async_copy(lab_hbm, lab_ref, small_sems.at[0])
    lab_copy.start()
    copies = []
    for b in range(PACK):
        to = pl.multiple_of(((b + turn) % PACK) * CAPR, CAPR)
        copies.append(pltpu.make_async_copy(x_ref.at[pl.ds(b * CAPR, CAPR)], frames_ref.at[pl.ds(to, CAPR)], sems.at[b]))
        copies.append(pltpu.make_async_copy(
            x_ref.at[pl.ds(LANES, CAPR)], frames_ref.at[pl.ds(LANES + b * CAPR, CAPR)], sems.at[PACK + b]))
    for copy in copies:
        copy.start()

    row = lax.broadcasted_iota(jnp.int32, (WIDE, WIDE), 0)
    col = lax.broadcasted_iota(jnp.int32, (WIDE, WIDE), 1)
    upper = (row < col).astype(jnp.bfloat16)
    lower = (col < row).astype(jnp.bfloat16)
    ones = jnp.ones((WIDE, LANES), jnp.bfloat16)
    blocks = part // WIDE
    lab_copy.wait()
    cycle = lab_ref[...]
    reader, inner = cycle // (CYCLES // readers), cycle % (CYCLES // readers)
    lab_ref[...] = ((inner // blks) * readers + reader) * blks + inner % blks
    member = jnp.concatenate(
        [(lab_ref[:, i * WIDE:(i + 1) * WIDE] == row).astype(jnp.bfloat16) for i in range(pixels // WIDE)], axis=0)
    earlier = dot(member, upper)
    counts = dot(member, ones)
    done = jnp.zeros((CYCLES, LANES), jnp.float32)
    for h in range(PARTS):
        count = [counts[i * CYCLES:(i + 1) * CYCLES] for i in range(h * blocks, (h + 1) * blocks)]
        total = functools.reduce(lambda a, b: a + b, count)
        base = dot(lower, total.astype(jnp.bfloat16))
        table_ref[2 * h:2 * h + 1, :] = (base - done + CAPR).T[:1].astype(jnp.int32)
        done = done + total
        table_ref[2 * h + 1:2 * h + 2, :] = done.T[:1].astype(jnp.int32)
        for i in range(blocks):
            at = h * part + i * WIDE
            from_row = (h * blocks + i) * CYCLES
            spot = earlier[from_row:from_row + CYCLES] + jnp.concatenate([base, base], axis=1)
            place_ref[:, at:at + WIDE] = jnp.sum(
                jnp.where(lab_ref[:, at:at + WIDE] == row, spot, 0.0), axis=0, keepdims=True)
            base = base + count[i]
    table_copy = pltpu.make_async_copy(table_ref, scalars, small_sems.at[1])
    table_copy.start()

    for copy in copies:
        copy.wait()
    spot = lax.broadcasted_iota(jnp.int32, (part, part), 0).astype(jnp.float32)
    block_of = lax.broadcasted_iota(jnp.int32, (CAPR + part, LANES), 1) // CAPR
    for h in range(PARTS):
        chosen = (spot == place_ref[:, h * part:(h + 1) * part]).astype(jnp.bfloat16)
        ordered = dot(chosen, frames_ref[:, h * part:(h + 1) * part], NT)
        main_ref[h, CAPR:CAPR + part, :] = ordered[:, :LANES]
        tail = jnp.concatenate([jnp.zeros((CAPR, LANES), jnp.float32), ordered[:, LANES:]], axis=0)
        folded = tail
        for q in range(1, PACK):
            shifted = jnp.concatenate([tail[q * SHORT:], tail[:q * SHORT]], axis=0)
            folded = jnp.where(block_of == q, shifted, folded)
        rest_ref[h, :CAPR + part, :] = folded

    table_copy.wait()
    slot = lax.broadcasted_iota(jnp.int32, (CAPR, LANES), 0)
    slot_rest = lax.broadcasted_iota(jnp.int32, (SHORT, LANES), 0) + SHORT * block_of[:SHORT]

    def spread(pair, carry):
        parts = []
        for odd in range(2):
            cycle = pair * 2 + odd
            main = jnp.zeros((CAPR, LANES), jnp.float32)
            rest = jnp.zeros((SHORT, LANES), jnp.float32)
            for h in reversed(range(PARTS)):
                at = scalars[2 * h, cycle]
                end = scalars[2 * h + 1, cycle]
                main = jnp.where(slot < end, main_ref[h, pl.ds(at, CAPR), :], main)
                rest = jnp.where(slot_rest < end, rest_ref[h, pl.ds(at, SHORT), :], rest)
            parts += [main, rest]
        to = pl.multiple_of(pair * (2 * ROWS), 2 * ROWS)
        send_ref[pl.ds(to, 2 * ROWS), :] = jnp.concatenate(parts, axis=0).astype(jnp.bfloat16)
        return carry

    pairs = CYCLES // 2 // CHUNKS
    outs = []
    for c in range(CHUNKS):
        lax.fori_loop(c * pairs, (c + 1) * pairs, spread, 0, unroll=4)
        rows = pl.ds(c * pairs * 2 * ROWS, pairs * 2 * ROWS)
        outs.append(pltpu.make_async_copy(send_ref.at[rows], out_ref.at[rows], out_sems.at[c]))
        outs[-1].start()
    for copy in outs:
        copy.wait()


def pick(intensity, labels, turn, readers=4, blks=8):
    pixels = intensity.shape[1]
    part = pixels // PARTS
    return pl.pallas_call(
        functools.partial(pick_kernel, readers, blks),
        in_specs=[
            pl.BlockSpec(memory_space=pltpu.SMEM),
            pl.BlockSpec(memory_space=pl.ANY),
            pl.BlockSpec(memory_space=pl.ANY),
        ],
        out_specs=pl.BlockSpec(memory_space=pl.ANY),
        out_shape=jax.ShapeDtypeStruct((CYCLES * ROWS, LANES), jnp.bfloat16),
        scratch_shapes=[
            pltpu.VMEM((1, pixels), jnp.int32),
            pltpu.VMEM((2 * LANES, pixels), jnp.bfloat16),
            pltpu.VMEM((1, pixels), jnp.float32),
            pltpu.VMEM((2 * PARTS, CYCLES), jnp.int32),
            pltpu.VMEM((PARTS, part + 2 * CAPR, LANES), jnp.float32),
            pltpu.VMEM((PARTS, part + 2 * CAPR, LANES), jnp.float32),
            pltpu.VMEM((CYCLES * ROWS, LANES), jnp.bfloat16),
            pltpu.SMEM((2 * PARTS, CYCLES), jnp.int32),
            pltpu.SemaphoreType.DMA((2 * PACK,)),
            pltpu.SemaphoreType.DMA((2,)),
            pltpu.SemaphoreType.DMA((CHUNKS,)),
        ],
        compiler_params=pltpu.CompilerParams(vmem_limit_bytes=60 * 2**20),
        name="pick_pixels",
    )(turn, labels.reshape(1, pixels), intensity)


def gram_kernel(blks, got_ref, out_ref, all_ref, hold_ref, sems):
    groups = all_ref.shape[0] // CAPR
    block_of = lax.broadcasted_iota(jnp.int32, (CAPR, LANES), 1) // CAPR
    filled = jnp.zeros((CAPR, LANES), jnp.float32)
    for g in range(0, groups, 2):
        got = []
        for r in range(PACK):
            at = ((g // blks * PACK + r) * blks + g % blks) * ROWS
            got.append(got_ref[at:at + 2 * ROWS, :].astype(jnp.float32))
        both = []
        for odd in range(2):
            m = [x[odd * ROWS:odd * ROWS + CAPR] for x in got]
            rest = swap_blocks(jnp.concatenate([x[odd * ROWS + CAPR:(odd + 1) * ROWS] for x in got], axis=0))
            filled = filled + (m[0] > 0).astype(jnp.float32)
            tiles = []
            for t in range(PACK + 1):
                tile = rest
                if t > 0:
                    tile = jnp.where(block_of < t - 1, m[t - 1], tile)
                if t < PACK:
                    tile = jnp.where(block_of >= t, m[t], tile)
                tiles.append(tile)
            both.append(jnp.concatenate(tiles, axis=1))
        all_ref[g * CAPR:(g + 2) * CAPR, :] = jnp.concatenate(both, axis=0).astype(jnp.bfloat16)
    series = all_ref[...]
    sums = dot(jnp.ones((8, series.shape[0]), jnp.bfloat16), series)
    count = jnp.sum(filled, axis=0, keepdims=True)[:, :1]
    left = count / sums.T[:, :1]
    right = 1.0 / sums[:1]
    outs = []
    total = series.shape[1]
    for t in range(0, total, TALL):
        rows = pl.ds(t, TALL)
        block = dot(all_ref[:, t:t + TALL], all_ref[:, t:], TN) * left[t:t + TALL] * right[:, t:]
        hold_ref[rows, t:] = block
        for u in range(t + TALL, total, TALL):
            hold_ref[u:u + TALL, t:t + TALL] = block[:, u - t:u - t + TALL].T
        outs.append(pltpu.make_async_copy(hold_ref.at[rows], out_ref.at[0, rows], sems.at[t // TALL]))
        outs[-1].start()
    for copy in outs:
        copy.wait()


def correlate(got, total, blks=8):
    slots = got.shape[0] * LANES // total
    return pl.pallas_call(
        functools.partial(gram_kernel, blks),
        out_shape=jax.ShapeDtypeStruct((1, total, total), jnp.float32),
        in_specs=[pl.BlockSpec(memory_space=pltpu.VMEM)],
        out_specs=pl.BlockSpec(memory_space=pl.ANY),
        scratch_shapes=[
            pltpu.VMEM((slots, total), jnp.bfloat16),
            pltpu.VMEM((total, total), jnp.float32),
            pltpu.SemaphoreType.DMA((total // TALL,)),
        ],
        compiler_params=pltpu.CompilerParams(vmem_limit_bytes=48 * 2**20),
        name="correlate",
    )(got)


def body(intensity, labels):
    turn = lax.axis_index("reader").astype(jnp.int32).reshape(1)
    readers, blks = lax.axis_size("reader"), lax.axis_size("blk")
    outgoing = pick(intensity, labels, turn, readers, blks)
    got = lax.all_to_all(outgoing, ROUTE, split_axis=0, concat_axis=0, tiled=True)
    return correlate(got, intensity.shape[0] * readers, blks)


def solution(mesh):
    placed = (P("reader", ("pixel", "blk")), P(("pixel", "blk"), None))
    return jax.shard_map(
        body,
        mesh=mesh,
        in_specs=placed,
        out_specs=P(AXES, None, None),
        check_vma=False,
    )
```

```python
import functools

import jax
import jax.numpy as jnp
from jax import lax
from jax.experimental import pallas as pl
from jax.experimental.pallas import tpu as pltpu
from jax.sharding import PartitionSpec as P

CYCLES = 256
CAPR = 32
AXES = ("reader", "pixel", "blk")
ROUTE = ("pixel", "reader", "blk")
LANES = 128
WIDE = 256
PACK = LANES // CAPR
SHORT = CAPR // PACK
ROWS = CAPR + SHORT
PARTS = 4
CHUNKS = 8
TALL = 128
NN = (((1,), (0,)), ((), ()))
NT = (((1,), (1,)), ((), ()))
TN = (((0,), (0,)), ((), ()))


def dot(a, b, dims=NN):
    return lax.dot_general(a, b, dims, preferred_element_type=jnp.float32)


def swap_blocks(tile):
    height = tile.shape[0] // PACK
    block_of = lax.broadcasted_iota(jnp.int32, (height, LANES), 1) // CAPR
    turned = []
    for a in range(PACK):
        part = tile[a * height:(a + 1) * height]
        turned.append(pltpu.roll(part, CAPR * a, 1) if a else part)
    out = []
    for b in range(PACK):
        merged = turned[(0 - b) % PACK]
        for j in range(1, PACK):
            merged = jnp.where(block_of == j, turned[(j - b) % PACK], merged)
        out.append(pltpu.roll(merged, LANES - CAPR * b, 1) if b else merged)
    return jnp.concatenate(out, axis=0)


def pick_kernel(readers, blks, turn_ref, lab_hbm, x_ref, out_ref, lab_ref, frames_ref, place_ref, table_ref, main_ref, rest_ref,
                send_ref, scalars, sems, small_sems, out_sems):
    pixels = x_ref.shape[1]
    part = pixels // PARTS
    turn = turn_ref[0]
    lab_copy = pltpu.make_async_copy(lab_hbm, lab_ref, small_sems.at[0])
    lab_copy.start()
    copies = []
    for b in range(PACK):
        to = pl.multiple_of(((b + turn) % PACK) * CAPR, CAPR)
        copies.append(pltpu.make_async_copy(x_ref.at[pl.ds(b * CAPR, CAPR)], frames_ref.at[pl.ds(to, CAPR)], sems.at[b]))
        copies.append(pltpu.make_async_copy(
            x_ref.at[pl.ds(LANES, CAPR)], frames_ref.at[pl.ds(LANES + b * CAPR, CAPR)], sems.at[PACK + b]))
    for copy in copies:
        copy.start()

    row = lax.broadcasted_iota(jnp.int32, (WIDE, WIDE), 0)
    col = lax.broadcasted_iota(jnp.int32, (WIDE, WIDE), 1)
    upper = (row < col).astype(jnp.bfloat16)
    lower = (col < row).astype(jnp.bfloat16)
    ones = jnp.ones((WIDE, LANES), jnp.bfloat16)
    blocks = part // WIDE
    lab_copy.wait()
    cycle = lab_ref[...]
    reader, inner = cycle // (CYCLES // readers), cycle % (CYCLES // readers)
    lab_ref[...] = ((inner // blks) * readers + reader) * blks + inner % blks
    member = jnp.concatenate(
        [(lab_ref[:, i * WIDE:(i + 1) * WIDE] == row).astype(jnp.bfloat16) for i in range(pixels // WIDE)], axis=0)
    earlier = dot(member, upper)
    done = jnp.zeros((CYCLES, LANES), jnp.float32)
    for h in range(PARTS):
        count = []
        for i in range(h * blocks, (h + 1) * blocks):
            last = earlier[i * CYCLES:(i + 1) * CYCLES, WIDE - 1:] + (lab_ref[:, (i + 1) * WIDE - 1:(i + 1) * WIDE] == row[:, :1]).astype(jnp.float32)
            count.append(jnp.broadcast_to(last, (CYCLES, LANES)))
        total = functools.reduce(lambda a, b: a + b, count)
        base = dot(lower, total.astype(jnp.bfloat16))
        table_ref[2 * h:2 * h + 1, :] = (base - done + CAPR).T[:1].astype(jnp.int32)
        done = done + total
        table_ref[2 * h + 1:2 * h + 2, :] = done.T[:1].astype(jnp.int32)
        for i in range(blocks):
            at = h * part + i * WIDE
            from_row = (h * blocks + i) * CYCLES
            spot = earlier[from_row:from_row + CYCLES] + jnp.concatenate([base, base], axis=1)
            place_ref[:, at:at + WIDE] = jnp.sum(
                jnp.where(lab_ref[:, at:at + WIDE] == row, spot, 0.0), axis=0, keepdims=True)
            base = base + count[i]
    table_copy = pltpu.make_async_copy(table_ref, scalars, small_sems.at[1])
    table_copy.start()

    for copy in copies:
        copy.wait()
    spot = lax.broadcasted_iota(jnp.int32, (part, part), 0).astype(jnp.float32)
    block_of = lax.broadcasted_iota(jnp.int32, (CAPR + part, LANES), 1) // CAPR
    for h in range(PARTS):
        chosen = (spot == place_ref[:, h * part:(h + 1) * part]).astype(jnp.bfloat16)
        ordered = dot(chosen, frames_ref[:, h * part:(h + 1) * part], NT)
        main_ref[h, CAPR:CAPR + part, :] = ordered[:, :LANES]
        tail = jnp.concatenate([jnp.zeros((CAPR, LANES), jnp.float32), ordered[:, LANES:]], axis=0)
        folded = tail
        for q in range(1, PACK):
            shifted = jnp.concatenate([tail[q * SHORT:], tail[:q * SHORT]], axis=0)
            folded = jnp.where(block_of == q, shifted, folded)
        rest_ref[h, :CAPR + part, :] = folded

    table_copy.wait()
    slot = lax.broadcasted_iota(jnp.int32, (CAPR, LANES), 0)
    slot_rest = lax.broadcasted_iota(jnp.int32, (SHORT, LANES), 0) + SHORT * block_of[:SHORT]

    def spread(pair, carry):
        parts = []
        for odd in range(2):
            cycle = pair * 2 + odd
            main = jnp.zeros((CAPR, LANES), jnp.float32)
            rest = jnp.zeros((SHORT, LANES), jnp.float32)
            for h in reversed(range(PARTS)):
                at = scalars[2 * h, cycle]
                end = scalars[2 * h + 1, cycle]
                main = jnp.where(slot < end, main_ref[h, pl.ds(at, CAPR), :], main)
                rest = jnp.where(slot_rest < end, rest_ref[h, pl.ds(at, SHORT), :], rest)
            parts += [main, rest]
        to = pl.multiple_of(pair * (2 * ROWS), 2 * ROWS)
        send_ref[pl.ds(to, 2 * ROWS), :] = jnp.concatenate(parts, axis=0).astype(jnp.bfloat16)
        return carry

    pairs = CYCLES // 2 // CHUNKS
    outs = []
    for c in range(CHUNKS):
        lax.fori_loop(c * pairs, (c + 1) * pairs, spread, 0, unroll=16)
        rows = pl.ds(c * pairs * 2 * ROWS, pairs * 2 * ROWS)
        outs.append(pltpu.make_async_copy(send_ref.at[rows], out_ref.at[rows], out_sems.at[c]))
        outs[-1].start()
    for copy in outs:
        copy.wait()


def pick(intensity, labels, turn, readers=4, blks=8):
    pixels = intensity.shape[1]
    part = pixels // PARTS
    return pl.pallas_call(
        functools.partial(pick_kernel, readers, blks),
        in_specs=[
            pl.BlockSpec(memory_space=pltpu.SMEM),
            pl.BlockSpec(memory_space=pl.ANY),
            pl.BlockSpec(memory_space=pl.ANY),
        ],
        out_specs=pl.BlockSpec(memory_space=pl.ANY),
        out_shape=jax.ShapeDtypeStruct((CYCLES * ROWS, LANES), jnp.bfloat16),
        scratch_shapes=[
            pltpu.VMEM((1, pixels), jnp.int32),
            pltpu.VMEM((2 * LANES, pixels), jnp.bfloat16),
            pltpu.VMEM((1, pixels), jnp.float32),
            pltpu.VMEM((2 * PARTS, CYCLES), jnp.int32),
            pltpu.VMEM((PARTS, part + 2 * CAPR, LANES), jnp.float32),
            pltpu.VMEM((PARTS, part + 2 * CAPR, LANES), jnp.float32),
            pltpu.VMEM((CYCLES * ROWS, LANES), jnp.bfloat16),
            pltpu.SMEM((2 * PARTS, CYCLES), jnp.int32),
            pltpu.SemaphoreType.DMA((2 * PACK,)),
            pltpu.SemaphoreType.DMA((2,)),
            pltpu.SemaphoreType.DMA((CHUNKS,)),
        ],
        compiler_params=pltpu.CompilerParams(vmem_limit_bytes=60 * 2**20),
        name="pick_pixels",
    )(turn, labels.reshape(1, pixels), intensity)


def gram_kernel(blks, got_ref, out_ref, all_ref, hold_ref, sems):
    groups = all_ref.shape[0] // CAPR
    block_of = lax.broadcasted_iota(jnp.int32, (CAPR, LANES), 1) // CAPR
    filled = jnp.zeros((CAPR, LANES), jnp.float32)
    for g in range(0, groups, 2):
        got = []
        for r in range(PACK):
            at = ((g // blks * PACK + r) * blks + g % blks) * ROWS
            got.append(got_ref[at:at + 2 * ROWS, :].astype(jnp.float32))
        both = []
        for odd in range(2):
            m = [x[odd * ROWS:odd * ROWS + CAPR] for x in got]
            rest = swap_blocks(jnp.concatenate([x[odd * ROWS + CAPR:(odd + 1) * ROWS] for x in got], axis=0))
            filled = filled + (m[0] > 0).astype(jnp.float32)
            tiles = []
            for t in range(PACK + 1):
                tile = rest
                if t > 0:
                    tile = jnp.where(block_of < t - 1, m[t - 1], tile)
                if t < PACK:
                    tile = jnp.where(block_of >= t, m[t], tile)
                tiles.append(tile)
            both.append(jnp.concatenate(tiles, axis=1))
        all_ref[g * CAPR:(g + 2) * CAPR, :] = jnp.concatenate(both, axis=0).astype(jnp.bfloat16)
    series = all_ref[...]
    sums = dot(jnp.ones((8, series.shape[0]), jnp.bfloat16), series)
    count = jnp.sum(filled, axis=0, keepdims=True)[:, :1]
    left = count / sums.T[:, :1]
    right = 1.0 / sums[:1]
    outs = []
    total = series.shape[1]
    for t in range(0, total, TALL):
        rows = pl.ds(t, TALL)
        block = dot(all_ref[:, t:t + TALL], all_ref[:, t:], TN) * left[t:t + TALL] * right[:, t:]
        hold_ref[rows, t:] = block
        for u in range(t + TALL, total, TALL):
            hold_ref[u:u + TALL, t:t + TALL] = block[:, u - t:u - t + TALL].T
        outs.append(pltpu.make_async_copy(hold_ref.at[rows], out_ref.at[0, rows], sems.at[t // TALL]))
        outs[-1].start()
    for copy in outs:
        copy.wait()


def correlate(got, total, blks=8):
    slots = got.shape[0] * LANES // total
    return pl.pallas_call(
        functools.partial(gram_kernel, blks),
        out_shape=jax.ShapeDtypeStruct((1, total, total), jnp.float32),
        in_specs=[pl.BlockSpec(memory_space=pltpu.VMEM)],
        out_specs=pl.BlockSpec(memory_space=pl.ANY),
        scratch_shapes=[
            pltpu.VMEM((slots, total), jnp.bfloat16),
            pltpu.VMEM((total, total), jnp.float32),
            pltpu.SemaphoreType.DMA((total // TALL,)),
        ],
        compiler_params=pltpu.CompilerParams(vmem_limit_bytes=48 * 2**20),
        name="correlate",
    )(got)


def body(intensity, labels):
    turn = lax.axis_index("reader").astype(jnp.int32).reshape(1)
    readers, blks = lax.axis_size("reader"), lax.axis_size("blk")
    outgoing = pick(intensity, labels, turn, readers, blks)
    got = lax.all_to_all(outgoing, ROUTE, split_axis=0, concat_axis=0, tiled=True)
    return correlate(got, intensity.shape[0] * readers, blks)


def solution(mesh):
    placed = (P("reader", ("pixel", "blk")), P(("pixel", "blk"), None))
    return jax.shard_map(
        body,
        mesh=mesh,
        in_specs=placed,
        out_specs=P(AXES, None, None),
        check_vma=False,
    )
```

```python
import functools

import jax
import jax.numpy as jnp
from jax import lax
from jax.experimental import pallas as pl
from jax.experimental.pallas import tpu as pltpu
from jax.sharding import PartitionSpec as P

CYCLES = 256
CAPR = 32
AXES = ("reader", "pixel", "blk")
ROUTE = ("pixel", "reader", "blk")
LANES = 128
WIDE = 256
PACK = LANES // CAPR
SHORT = CAPR // PACK
ROWS = CAPR + SHORT
PARTS = 4
CHUNKS = 8
TALL = 128
NN = (((1,), (0,)), ((), ()))
NT = (((1,), (1,)), ((), ()))
TN = (((0,), (0,)), ((), ()))


def dot(a, b, dims=NN):
    return lax.dot_general(a, b, dims, preferred_element_type=jnp.float32)


def swap_blocks(tile):
    height = tile.shape[0] // PACK
    block_of = lax.broadcasted_iota(jnp.int32, (height, LANES), 1) // CAPR
    turned = []
    for a in range(PACK):
        part = tile[a * height:(a + 1) * height]
        turned.append(pltpu.roll(part, CAPR * a, 1) if a else part)
    out = []
    for b in range(PACK):
        merged = turned[(0 - b) % PACK]
        for j in range(1, PACK):
            merged = jnp.where(block_of == j, turned[(j - b) % PACK], merged)
        out.append(pltpu.roll(merged, LANES - CAPR * b, 1) if b else merged)
    return jnp.concatenate(out, axis=0)


def pick_kernel(readers, blks, turn_ref, lab_hbm, x_ref, out_ref, lab_ref, frames_ref, place_ref, table_ref, main_ref, rest_ref,
                send_ref, scalars, sems, small_sems, out_sems):
    pixels = x_ref.shape[1]
    part = pixels // PARTS
    turn = turn_ref[0]
    lab_copy = pltpu.make_async_copy(lab_hbm, lab_ref, small_sems.at[0])
    lab_copy.start()
    copies = []
    for b in range(PACK):
        to = pl.multiple_of(((b + turn) % PACK) * CAPR, CAPR)
        copies.append(pltpu.make_async_copy(x_ref.at[pl.ds(b * CAPR, CAPR)], frames_ref.at[pl.ds(to, CAPR)], sems.at[b]))
    copies.append(pltpu.make_async_copy(x_ref.at[pl.ds(LANES, CAPR)], frames_ref.at[pl.ds(LANES, CAPR)], sems.at[PACK]))
    for copy in copies:
        copy.start()

    row = lax.broadcasted_iota(jnp.int32, (WIDE, WIDE), 0)
    col = lax.broadcasted_iota(jnp.int32, (WIDE, WIDE), 1)
    line = row // blks
    name = (line % readers) * (CYCLES // readers) + (line // readers) * blks + row % blks
    upper = (row < col).astype(jnp.bfloat16)
    lower = (col < row).astype(jnp.bfloat16)
    ones = jnp.ones((WIDE, LANES), jnp.bfloat16)
    blocks = part // WIDE
    lab_copy.wait()
    member = jnp.concatenate(
        [(lab_ref[:, i * WIDE:(i + 1) * WIDE] == name).astype(jnp.bfloat16) for i in range(pixels // WIDE)], axis=0)
    earlier = dot(member, upper)
    done = jnp.zeros((CYCLES, LANES), jnp.float32)
    for h in range(PARTS):
        count = []
        for i in range(h * blocks, (h + 1) * blocks):
            last = earlier[i * CYCLES:(i + 1) * CYCLES, WIDE - 1:] + (lab_ref[:, (i + 1) * WIDE - 1:(i + 1) * WIDE] == name[:, :1]).astype(jnp.float32)
            count.append(jnp.broadcast_to(last, (CYCLES, LANES)))
        total = functools.reduce(lambda a, b: a + b, count)
        base = dot(lower, total.astype(jnp.bfloat16))
        table_ref[2 * h:2 * h + 1, :] = (base - done + CAPR).T[:1].astype(jnp.int32)
        done = done + total
        table_ref[2 * h + 1:2 * h + 2, :] = done.T[:1].astype(jnp.int32)
        for i in range(blocks):
            at = h * part + i * WIDE
            from_row = (h * blocks + i) * CYCLES
            spot = earlier[from_row:from_row + CYCLES] + jnp.concatenate([base, base], axis=1)
            place_ref[:, at:at + WIDE] = jnp.sum(
                jnp.where(lab_ref[:, at:at + WIDE] == name, spot, 0.0), axis=0, keepdims=True)
            base = base + count[i]
    table_copy = pltpu.make_async_copy(table_ref, scalars, small_sems.at[1])
    table_copy.start()

    for copy in copies:
        copy.wait()
    for b in range(1, PACK):
        frames_ref[LANES + b * CAPR:LANES + (b + 1) * CAPR, :] = frames_ref[LANES:LANES + CAPR, :]
    spot = lax.broadcasted_iota(jnp.int32, (part, part), 0).astype(jnp.float32)
    block_of = lax.broadcasted_iota(jnp.int32, (CAPR + part, LANES), 1) // CAPR
    for h in range(PARTS):
        chosen = (spot == place_ref[:, h * part:(h + 1) * part]).astype(jnp.bfloat16)
        ordered = dot(chosen, frames_ref[:, h * part:(h + 1) * part], NT)
        main_ref[h, CAPR:CAPR + part, :] = ordered[:, :LANES]
        tail = jnp.concatenate([jnp.zeros((CAPR, LANES), jnp.float32), ordered[:, LANES:]], axis=0)
        folded = tail
        for q in range(1, PACK):
            shifted = jnp.concatenate([tail[q * SHORT:], tail[:q * SHORT]], axis=0)
            folded = jnp.where(block_of == q, shifted, folded)
        rest_ref[h, :CAPR + part, :] = folded

    table_copy.wait()
    slot = lax.broadcasted_iota(jnp.int32, (CAPR, LANES), 0)
    slot_rest = lax.broadcasted_iota(jnp.int32, (SHORT, LANES), 0) + SHORT * block_of[:SHORT]

    def spread(pair, carry):
        parts = []
        for odd in range(2):
            cycle = pair * 2 + odd
            main = jnp.zeros((CAPR, LANES), jnp.float32)
            rest = jnp.zeros((SHORT, LANES), jnp.float32)
            for h in reversed(range(PARTS)):
                at = scalars[2 * h, cycle]
                end = scalars[2 * h + 1, cycle]
                main = jnp.where(slot < end, main_ref[h, pl.ds(at, CAPR), :], main)
                rest = jnp.where(slot_rest < end, rest_ref[h, pl.ds(at, SHORT), :], rest)
            parts += [main, rest]
        to = pl.multiple_of(pair * (2 * ROWS), 2 * ROWS)
        send_ref[pl.ds(to, 2 * ROWS), :] = jnp.concatenate(parts, axis=0).astype(jnp.bfloat16)
        return carry

    pairs = CYCLES // 2 // CHUNKS
    outs = []
    for c in range(CHUNKS):
        lax.fori_loop(c * pairs, (c + 1) * pairs, spread, 0, unroll=16)
        rows = pl.ds(c * pairs * 2 * ROWS, pairs * 2 * ROWS)
        outs.append(pltpu.make_async_copy(send_ref.at[rows], out_ref.at[rows], out_sems.at[c]))
        outs[-1].start()
    for copy in outs:
        copy.wait()


def pick(intensity, labels, turn, readers=4, blks=8):
    pixels = intensity.shape[1]
    part = pixels // PARTS
    return pl.pallas_call(
        functools.partial(pick_kernel, readers, blks),
        in_specs=[
            pl.BlockSpec(memory_space=pltpu.SMEM),
            pl.BlockSpec(memory_space=pl.ANY),
            pl.BlockSpec(memory_space=pl.ANY),
        ],
        out_specs=pl.BlockSpec(memory_space=pl.ANY),
        out_shape=jax.ShapeDtypeStruct((CYCLES * ROWS, LANES), jnp.bfloat16),
        scratch_shapes=[
            pltpu.VMEM((1, pixels), jnp.int32),
            pltpu.VMEM((2 * LANES, pixels), jnp.bfloat16),
            pltpu.VMEM((1, pixels), jnp.float32),
            pltpu.VMEM((2 * PARTS, CYCLES), jnp.int32),
            pltpu.VMEM((PARTS, part + 2 * CAPR, LANES), jnp.float32),
            pltpu.VMEM((PARTS, part + 2 * CAPR, LANES), jnp.float32),
            pltpu.VMEM((CYCLES * ROWS, LANES), jnp.bfloat16),
            pltpu.SMEM((2 * PARTS, CYCLES), jnp.int32),
            pltpu.SemaphoreType.DMA((2 * PACK,)),
            pltpu.SemaphoreType.DMA((2,)),
            pltpu.SemaphoreType.DMA((CHUNKS,)),
        ],
        compiler_params=pltpu.CompilerParams(vmem_limit_bytes=60 * 2**20),
        name="pick_pixels",
    )(turn, labels.reshape(1, pixels), intensity)


def gram_kernel(blks, got_ref, out_ref, all_ref, hold_ref, sems):
    groups = all_ref.shape[0] // CAPR
    block_of = lax.broadcasted_iota(jnp.int32, (CAPR, LANES), 1) // CAPR
    filled = jnp.zeros((CAPR, LANES), jnp.float32)
    for g in range(0, groups, 2):
        got = []
        for r in range(PACK):
            at = ((g // blks * PACK + r) * blks + g % blks) * ROWS
            got.append(got_ref[at:at + 2 * ROWS, :].astype(jnp.float32))
        both = []
        for odd in range(2):
            m = [x[odd * ROWS:odd * ROWS + CAPR] for x in got]
            rest = swap_blocks(jnp.concatenate([x[odd * ROWS + CAPR:(odd + 1) * ROWS] for x in got], axis=0))
            filled = filled + (m[0] > 0).astype(jnp.float32)
            tiles = []
            for t in range(PACK + 1):
                tile = rest
                if t > 0:
                    tile = jnp.where(block_of < t - 1, m[t - 1], tile)
                if t < PACK:
                    tile = jnp.where(block_of >= t, m[t], tile)
                tiles.append(tile)
            both.append(jnp.concatenate(tiles, axis=1))
        all_ref[g * CAPR:(g + 2) * CAPR, :] = jnp.concatenate(both, axis=0).astype(jnp.bfloat16)
    series = all_ref[...]
    sums = dot(jnp.ones((8, series.shape[0]), jnp.bfloat16), series)
    count = jnp.sum(filled, axis=0, keepdims=True)[:, :1]
    left = count / sums.T[:, :1]
    right = 1.0 / sums[:1]
    outs = []
    total = series.shape[1]
    for t in range(0, total, TALL):
        rows = pl.ds(t, TALL)
        block = dot(all_ref[:, t:t + TALL], all_ref[:, t:], TN) * left[t:t + TALL] * right[:, t:]
        hold_ref[rows, t:] = block
        for u in range(t + TALL, total, TALL):
            hold_ref[u:u + TALL, t:t + TALL] = block[:, u - t:u - t + TALL].T
        outs.append(pltpu.make_async_copy(hold_ref.at[rows], out_ref.at[0, rows], sems.at[t // TALL]))
        outs[-1].start()
    for copy in outs:
        copy.wait()


def correlate(got, total, blks=8):
    slots = got.shape[0] * LANES // total
    return pl.pallas_call(
        functools.partial(gram_kernel, blks),
        out_shape=jax.ShapeDtypeStruct((1, total, total), jnp.float32),
        in_specs=[pl.BlockSpec(memory_space=pltpu.VMEM)],
        out_specs=pl.BlockSpec(memory_space=pl.ANY),
        scratch_shapes=[
            pltpu.VMEM((slots, total), jnp.bfloat16),
            pltpu.VMEM((total, total), jnp.float32),
            pltpu.SemaphoreType.DMA((total // TALL,)),
        ],
        compiler_params=pltpu.CompilerParams(vmem_limit_bytes=48 * 2**20),
        name="correlate",
    )(got)


def body(intensity, labels):
    turn = lax.axis_index("reader").astype(jnp.int32).reshape(1)
    readers, blks = lax.axis_size("reader"), lax.axis_size("blk")
    outgoing = pick(intensity, labels, turn, readers, blks)
    got = lax.all_to_all(outgoing, ROUTE, split_axis=0, concat_axis=0, tiled=True)
    return correlate(got, intensity.shape[0] * readers, blks)


def solution(mesh):
    placed = (P("reader", ("pixel", "blk")), P(("pixel", "blk"), None))
    return jax.shard_map(
        body,
        mesh=mesh,
        in_specs=placed,
        out_specs=P(AXES, None, None),
        check_vma=False,
    )
```

```python
import functools

import jax
import jax.numpy as jnp
from jax import lax
from jax.experimental import pallas as pl
from jax.experimental.pallas import tpu as pltpu
from jax.sharding import PartitionSpec as P

CYCLES = 256
CAPR = 32
AXES = ("reader", "pixel", "blk")
ROUTE = ("pixel", "reader", "blk")
LANES = 128
WIDE = 256
PACK = LANES // CAPR
SHORT = CAPR // PACK
ROWS = CAPR + SHORT
PARTS = 4
CHUNKS = 8
GROUP = 8
TALL = 128
NN = (((1,), (0,)), ((), ()))
NT = (((1,), (1,)), ((), ()))
TN = (((0,), (0,)), ((), ()))


def dot(a, b, dims=NN):
    return lax.dot_general(a, b, dims, preferred_element_type=jnp.float32)


def swap_blocks(tile):
    height = tile.shape[0] // PACK
    block_of = lax.broadcasted_iota(jnp.int32, (height, LANES), 1) // CAPR
    turned = []
    for a in range(PACK):
        part = tile[a * height:(a + 1) * height]
        turned.append(pltpu.roll(part, CAPR * a, 1) if a else part)
    out = []
    for b in range(PACK):
        merged = turned[(0 - b) % PACK]
        for j in range(1, PACK):
            merged = jnp.where(block_of == j, turned[(j - b) % PACK], merged)
        out.append(pltpu.roll(merged, LANES - CAPR * b, 1) if b else merged)
    return jnp.concatenate(out, axis=0)


def pick_kernel(readers, blks, lab_hbm, x_ref, out_ref, lab_ref, frames_ref, place_ref, table_ref, main_ref, rest_ref,
                send_ref, scalars, sems, small_sems, out_sems):
    pixels = x_ref.shape[1]
    part = pixels // PARTS
    turn = lax.axis_index("reader")
    lab_copy = pltpu.make_async_copy(lab_hbm, lab_ref, small_sems.at[0])
    lab_copy.start()
    copies = []
    for b in range(PACK):
        to = pl.multiple_of(((b + turn) % PACK) * CAPR, CAPR)
        copies.append(pltpu.make_async_copy(x_ref.at[pl.ds(b * CAPR, CAPR)], frames_ref.at[pl.ds(to, CAPR)], sems.at[b]))
    copies.append(pltpu.make_async_copy(x_ref.at[pl.ds(LANES, CAPR)], frames_ref.at[pl.ds(LANES, CAPR)], sems.at[PACK]))

    row = lax.broadcasted_iota(jnp.int32, (WIDE, WIDE), 0)
    col = lax.broadcasted_iota(jnp.int32, (WIDE, WIDE), 1)
    line = row // blks
    name = (line % readers) * (CYCLES // readers) + (line // readers) * blks + row % blks
    upper = (row < col).astype(jnp.bfloat16)
    lower = (col < row).astype(jnp.bfloat16)
    ones = jnp.ones((WIDE, LANES), jnp.bfloat16)
    blocks = part // WIDE
    lab_copy.wait()
    for copy in copies:
        copy.start()
    earliers = []
    for begin in range(0, pixels // WIDE, GROUP):
        member = jnp.concatenate(
            [(lab_ref[:, i * WIDE:(i + 1) * WIDE] == name).astype(jnp.bfloat16) for i in range(begin, begin + GROUP)], axis=0)
        earliers.append(dot(member, upper))
    earlier = jnp.concatenate(earliers, axis=0)
    done = jnp.zeros((CYCLES, LANES), jnp.float32)
    for h in range(PARTS):
        count = []
        for i in range(h * blocks, (h + 1) * blocks):
            last = earlier[i * CYCLES:(i + 1) * CYCLES, WIDE - 1:] + (lab_ref[:, (i + 1) * WIDE - 1:(i + 1) * WIDE] == name[:, :1]).astype(jnp.float32)
            count.append(jnp.broadcast_to(last, (CYCLES, LANES)))
        total = functools.reduce(lambda a, b: a + b, count)
        base = dot(lower, total.astype(jnp.bfloat16))
        table_ref[2 * h:2 * h + 1, :] = (base - done + CAPR).T[:1].astype(jnp.int32)
        done = done + total
        table_ref[2 * h + 1:2 * h + 2, :] = done.T[:1].astype(jnp.int32)
        for i in range(blocks):
            at = h * part + i * WIDE
            from_row = (h * blocks + i) * CYCLES
            spot = earlier[from_row:from_row + CYCLES] + jnp.concatenate([base, base], axis=1)
            place_ref[:, at:at + WIDE] = jnp.sum(
                jnp.where(lab_ref[:, at:at + WIDE] == name, spot, 0.0), axis=0, keepdims=True)
            base = base + count[i]
    table_copy = pltpu.make_async_copy(table_ref, scalars, small_sems.at[1])
    table_copy.start()

    for copy in copies:
        copy.wait()
    for b in range(1, PACK):
        frames_ref[LANES + b * CAPR:LANES + (b + 1) * CAPR, :] = frames_ref[LANES:LANES + CAPR, :]
    spot = lax.broadcasted_iota(jnp.int32, (part, part), 0).astype(jnp.float32)
    block_of = lax.broadcasted_iota(jnp.int32, (CAPR + part, LANES), 1) // CAPR
    for h in range(PARTS):
        chosen = (spot == place_ref[:, h * part:(h + 1) * part]).astype(jnp.bfloat16)
        ordered = dot(chosen, frames_ref[:, h * part:(h + 1) * part], NT)
        main_ref[h, CAPR:CAPR + part, :] = ordered[:, :LANES]
        tail = jnp.concatenate([jnp.zeros((CAPR, LANES), jnp.float32), ordered[:, LANES:]], axis=0)
        folded = tail
        for q in range(1, PACK):
            shifted = jnp.concatenate([tail[q * SHORT:], tail[:q * SHORT]], axis=0)
            folded = jnp.where(block_of == q, shifted, folded)
        rest_ref[h, :CAPR + part, :] = folded

    table_copy.wait()
    slot = lax.broadcasted_iota(jnp.int32, (CAPR, LANES), 0)
    slot_rest = lax.broadcasted_iota(jnp.int32, (SHORT, LANES), 0) + SHORT * block_of[:SHORT]

    def spread(pair, carry):
        parts = []
        for odd in range(2):
            cycle = pair * 2 + odd
            main = jnp.zeros((CAPR, LANES), jnp.float32)
            rest = jnp.zeros((SHORT, LANES), jnp.float32)
            for h in reversed(range(PARTS)):
                at = scalars[2 * h, cycle]
                end = scalars[2 * h + 1, cycle]
                main = jnp.where(slot < end, main_ref[h, pl.ds(at, CAPR), :], main)
                rest = jnp.where(slot_rest < end, rest_ref[h, pl.ds(at, SHORT), :], rest)
            parts += [main, rest]
        to = pl.multiple_of(pair * (2 * ROWS), 2 * ROWS)
        send_ref[pl.ds(to, 2 * ROWS), :] = jnp.concatenate(parts, axis=0).astype(jnp.bfloat16)
        return carry

    pairs = CYCLES // 2 // CHUNKS
    outs = []
    for c in range(CHUNKS):
        lax.fori_loop(c * pairs, (c + 1) * pairs, spread, 0, unroll=16)
        rows = pl.ds(c * pairs * 2 * ROWS, pairs * 2 * ROWS)
        outs.append(pltpu.make_async_copy(send_ref.at[rows], out_ref.at[rows], out_sems.at[c]))
        outs[-1].start()
    for copy in outs:
        copy.wait()


def pick(intensity, labels, readers=4, blks=8):
    pixels = intensity.shape[1]
    part = pixels // PARTS
    return pl.pallas_call(
        functools.partial(pick_kernel, readers, blks),
        in_specs=[
            pl.BlockSpec(memory_space=pl.ANY),
            pl.BlockSpec(memory_space=pl.ANY),
        ],
        out_specs=pl.BlockSpec(memory_space=pl.ANY),
        out_shape=jax.ShapeDtypeStruct((CYCLES * ROWS, LANES), jnp.bfloat16),
        scratch_shapes=[
            pltpu.VMEM((1, pixels), jnp.int32),
            pltpu.VMEM((2 * LANES, pixels), jnp.bfloat16),
            pltpu.VMEM((1, pixels), jnp.float32),
            pltpu.VMEM((2 * PARTS, CYCLES), jnp.int32),
            pltpu.VMEM((PARTS, part + 2 * CAPR, LANES), jnp.float32),
            pltpu.VMEM((PARTS, part + 2 * CAPR, LANES), jnp.float32),
            pltpu.VMEM((CYCLES * ROWS, LANES), jnp.bfloat16),
            pltpu.SMEM((2 * PARTS, CYCLES), jnp.int32),
            pltpu.SemaphoreType.DMA((2 * PACK,)),
            pltpu.SemaphoreType.DMA((2,)),
            pltpu.SemaphoreType.DMA((CHUNKS,)),
        ],
        compiler_params=pltpu.CompilerParams(vmem_limit_bytes=60 * 2**20),
        name="pick_pixels",
    )(labels.reshape(1, pixels), intensity)


def gram_kernel(blks, got_ref, out_ref, all_ref, hold_ref, sems):
    groups = all_ref.shape[0] // CAPR
    block_of = lax.broadcasted_iota(jnp.int32, (CAPR, LANES), 1) // CAPR
    filled = jnp.zeros((CAPR, LANES), jnp.float32)
    for g in range(0, groups, 2):
        got = []
        for r in range(PACK):
            at = ((g // blks * PACK + r) * blks + g % blks) * ROWS
            got.append(got_ref[at:at + 2 * ROWS, :].astype(jnp.float32))
        both = []
        for odd in range(2):
            m = [x[odd * ROWS:odd * ROWS + CAPR] for x in got]
            rest = swap_blocks(jnp.concatenate([x[odd * ROWS + CAPR:(odd + 1) * ROWS] for x in got], axis=0))
            filled = filled + (m[0] > 0).astype(jnp.float32)
            tiles = []
            for t in range(PACK + 1):
                tile = rest
                if t > 0:
                    tile = jnp.where(block_of < t - 1, m[t - 1], tile)
                if t < PACK:
                    tile = jnp.where(block_of >= t, m[t], tile)
                tiles.append(tile)
            both.append(jnp.concatenate(tiles, axis=1))
        all_ref[g * CAPR:(g + 2) * CAPR, :] = jnp.concatenate(both, axis=0).astype(jnp.bfloat16)
    series = all_ref[...]
    sums = dot(jnp.ones((8, series.shape[0]), jnp.bfloat16), series)
    count = jnp.sum(filled, axis=0, keepdims=True)[:, :1]
    left = count / sums.T[:, :1]
    right = 1.0 / sums[:1]
    outs = []
    total = series.shape[1]
    for t in range(0, total, TALL):
        rows = pl.ds(t, TALL)
        block = dot(all_ref[:, t:t + TALL], all_ref[:, t:], TN) * left[t:t + TALL] * right[:, t:]
        hold_ref[rows, t:] = block
        for u in range(t + TALL, total, TALL):
            hold_ref[u:u + TALL, t:t + TALL] = block[:, u - t:u - t + TALL].T
        outs.append(pltpu.make_async_copy(hold_ref.at[rows], out_ref.at[0, rows], sems.at[t // TALL]))
        outs[-1].start()
    for copy in outs:
        copy.wait()


def correlate(got, total, blks=8):
    slots = got.shape[0] * LANES // total
    return pl.pallas_call(
        functools.partial(gram_kernel, blks),
        out_shape=jax.ShapeDtypeStruct((1, total, total), jnp.float32),
        in_specs=[pl.BlockSpec(memory_space=pltpu.VMEM)],
        out_specs=pl.BlockSpec(memory_space=pl.ANY),
        scratch_shapes=[
            pltpu.VMEM((slots, total), jnp.bfloat16),
            pltpu.VMEM((total, total), jnp.float32),
            pltpu.SemaphoreType.DMA((total // TALL,)),
        ],
        compiler_params=pltpu.CompilerParams(vmem_limit_bytes=48 * 2**20),
        name="correlate",
    )(got)


def body(intensity, labels):
    readers, blks = lax.axis_size("reader"), lax.axis_size("blk")
    outgoing = pick(intensity, labels, readers, blks)
    got = lax.all_to_all(outgoing, ROUTE, split_axis=0, concat_axis=0, tiled=True)
    return correlate(got, intensity.shape[0] * readers, blks)


def solution(mesh):
    placed = (P("reader", ("pixel", "blk")), P(("pixel", "blk"), None))
    return jax.shard_map(
        body,
        mesh=mesh,
        in_specs=placed,
        out_specs=P(AXES, None, None),
        check_vma=False,
    )
```

```python
import functools

import jax
import jax.numpy as jnp
from jax import lax
from jax.experimental import pallas as pl
from jax.experimental.pallas import tpu as pltpu
from jax.sharding import PartitionSpec as P

CYCLES = 256
CAPR = 32
AXES = ("reader", "pixel", "blk")
ROUTE = ("blk", "reader", "pixel")
LANES = 128
WIDE = 256
PACK = LANES // CAPR
SHORT = CAPR // PACK
ROWS = CAPR + SHORT
PARTS = 4
CHUNKS = 8
GROUP = 8
TALL = 128
NN = (((1,), (0,)), ((), ()))
NT = (((1,), (1,)), ((), ()))
TN = (((0,), (0,)), ((), ()))


def dot(a, b, dims=NN):
    return lax.dot_general(a, b, dims, preferred_element_type=jnp.float32)


def swap_blocks(tile):
    height = tile.shape[0] // PACK
    block_of = lax.broadcasted_iota(jnp.int32, (height, LANES), 1) // CAPR
    turned = []
    for a in range(PACK):
        part = tile[a * height:(a + 1) * height]
        turned.append(pltpu.roll(part, CAPR * a, 1) if a else part)
    out = []
    for b in range(PACK):
        merged = turned[(0 - b) % PACK]
        for j in range(1, PACK):
            merged = jnp.where(block_of == j, turned[(j - b) % PACK], merged)
        out.append(pltpu.roll(merged, LANES - CAPR * b, 1) if b else merged)
    return jnp.concatenate(out, axis=0)


def pick_kernel(readers, blks, lab_hbm, x_ref, out_ref, lab_ref, frames_ref, place_ref, table_ref, main_ref, rest_ref,
                send_ref, scalars, sems, small_sems, out_sems):
    pixels = x_ref.shape[1]
    part = pixels // PARTS
    turn = lax.axis_index("reader")
    lab_copy = pltpu.make_async_copy(lab_hbm, lab_ref, small_sems.at[0])
    lab_copy.start()
    copies = []
    for b in range(PACK):
        to = pl.multiple_of(((b + turn) % PACK) * CAPR, CAPR)
        copies.append(pltpu.make_async_copy(x_ref.at[pl.ds(b * CAPR, CAPR)], frames_ref.at[pl.ds(to, CAPR)], sems.at[b]))
    copies.append(pltpu.make_async_copy(x_ref.at[pl.ds(LANES, CAPR)], frames_ref.at[pl.ds(LANES, CAPR)], sems.at[PACK]))

    row = lax.broadcasted_iota(jnp.int32, (WIDE, WIDE), 0)
    col = lax.broadcasted_iota(jnp.int32, (WIDE, WIDE), 1)
    lots = CYCLES // (readers * blks)
    line = row // lots
    name = (line % readers) * (CYCLES // readers) + (row % lots) * blks + line // readers
    upper = (row < col).astype(jnp.bfloat16)
    lower = (col < row).astype(jnp.bfloat16)
    ones = jnp.ones((WIDE, LANES), jnp.bfloat16)
    blocks = part // WIDE
    lab_copy.wait()
    for copy in copies:
        copy.start()
    earliers = []
    for begin in range(0, pixels // WIDE, GROUP):
        member = jnp.concatenate(
            [(lab_ref[:, i * WIDE:(i + 1) * WIDE] == name).astype(jnp.bfloat16) for i in range(begin, begin + GROUP)], axis=0)
        earliers.append(dot(member, upper))
    earlier = jnp.concatenate(earliers, axis=0)
    done = jnp.zeros((CYCLES, LANES), jnp.float32)
    for h in range(PARTS):
        count = []
        for i in range(h * blocks, (h + 1) * blocks):
            last = earlier[i * CYCLES:(i + 1) * CYCLES, WIDE - 1:] + (lab_ref[:, (i + 1) * WIDE - 1:(i + 1) * WIDE] == name[:, :1]).astype(jnp.float32)
            count.append(jnp.broadcast_to(last, (CYCLES, LANES)))
        total = functools.reduce(lambda a, b: a + b, count)
        base = dot(lower, total.astype(jnp.bfloat16))
        table_ref[2 * h:2 * h + 1, :] = (base - done + CAPR).T[:1].astype(jnp.int32)
        done = done + total
        table_ref[2 * h + 1:2 * h + 2, :] = done.T[:1].astype(jnp.int32)
        for i in range(blocks):
            at = h * part + i * WIDE
            from_row = (h * blocks + i) * CYCLES
            spot = earlier[from_row:from_row + CYCLES] + jnp.concatenate([base, base], axis=1)
            place_ref[:, at:at + WIDE] = jnp.sum(
                jnp.where(lab_ref[:, at:at + WIDE] == name, spot, 0.0), axis=0, keepdims=True)
            base = base + count[i]
    table_copy = pltpu.make_async_copy(table_ref, scalars, small_sems.at[1])
    table_copy.start()

    for copy in copies:
        copy.wait()
    for b in range(1, PACK):
        frames_ref[LANES + b * CAPR:LANES + (b + 1) * CAPR, :] = frames_ref[LANES:LANES + CAPR, :]
    spot = lax.broadcasted_iota(jnp.int32, (part, part), 0).astype(jnp.float32)
    block_of = lax.broadcasted_iota(jnp.int32, (CAPR + part, LANES), 1) // CAPR
    for h in range(PARTS):
        chosen = (spot == place_ref[:, h * part:(h + 1) * part]).astype(jnp.bfloat16)
        ordered = dot(chosen, frames_ref[:, h * part:(h + 1) * part], NT)
        main_ref[h, CAPR:CAPR + part, :] = ordered[:, :LANES]
        tail = jnp.concatenate([jnp.zeros((CAPR, LANES), jnp.float32), ordered[:, LANES:]], axis=0)
        folded = tail
        for q in range(1, PACK):
            shifted = jnp.concatenate([tail[q * SHORT:], tail[:q * SHORT]], axis=0)
            folded = jnp.where(block_of == q, shifted, folded)
        rest_ref[h, :CAPR + part, :] = folded

    table_copy.wait()
    slot = lax.broadcasted_iota(jnp.int32, (CAPR, LANES), 0)
    slot_rest = lax.broadcasted_iota(jnp.int32, (SHORT, LANES), 0) + SHORT * block_of[:SHORT]

    def spread(pair, carry):
        parts = []
        for odd in range(2):
            cycle = pair * 2 + odd
            main = jnp.zeros((CAPR, LANES), jnp.float32)
            rest = jnp.zeros((SHORT, LANES), jnp.float32)
            for h in reversed(range(PARTS)):
                at = scalars[2 * h, cycle]
                end = scalars[2 * h + 1, cycle]
                main = jnp.where(slot < end, main_ref[h, pl.ds(at, CAPR), :], main)
                rest = jnp.where(slot_rest < end, rest_ref[h, pl.ds(at, SHORT), :], rest)
            parts += [main, rest]
        to = pl.multiple_of(pair * (2 * ROWS), 2 * ROWS)
        send_ref[pl.ds(to, 2 * ROWS), :] = jnp.concatenate(parts, axis=0).astype(jnp.bfloat16)
        return carry

    pairs = CYCLES // 2 // CHUNKS
    outs = []
    for c in range(CHUNKS):
        lax.fori_loop(c * pairs, (c + 1) * pairs, spread, 0, unroll=16)
        rows = pl.ds(c * pairs * 2 * ROWS, pairs * 2 * ROWS)
        outs.append(pltpu.make_async_copy(send_ref.at[rows], out_ref.at[rows], out_sems.at[c]))
        outs[-1].start()
    for copy in outs:
        copy.wait()


def pick(intensity, labels, readers=4, blks=8):
    pixels = intensity.shape[1]
    part = pixels // PARTS
    return pl.pallas_call(
        functools.partial(pick_kernel, readers, blks),
        in_specs=[
            pl.BlockSpec(memory_space=pl.ANY),
            pl.BlockSpec(memory_space=pl.ANY),
        ],
        out_specs=pl.BlockSpec(memory_space=pl.ANY),
        out_shape=jax.ShapeDtypeStruct((CYCLES * ROWS, LANES), jnp.bfloat16),
        scratch_shapes=[
            pltpu.VMEM((1, pixels), jnp.int32),
            pltpu.VMEM((2 * LANES, pixels), jnp.bfloat16),
            pltpu.VMEM((1, pixels), jnp.float32),
            pltpu.VMEM((2 * PARTS, CYCLES), jnp.int32),
            pltpu.VMEM((PARTS, part + 2 * CAPR, LANES), jnp.float32),
            pltpu.VMEM((PARTS, part + 2 * CAPR, LANES), jnp.float32),
            pltpu.VMEM((CYCLES * ROWS, LANES), jnp.bfloat16),
            pltpu.SMEM((2 * PARTS, CYCLES), jnp.int32),
            pltpu.SemaphoreType.DMA((2 * PACK,)),
            pltpu.SemaphoreType.DMA((2,)),
            pltpu.SemaphoreType.DMA((CHUNKS,)),
        ],
        compiler_params=pltpu.CompilerParams(vmem_limit_bytes=60 * 2**20),
        name="pick_pixels",
    )(labels.reshape(1, pixels), intensity)


def gram_kernel(lots, got_ref, out_ref, all_ref, hold_ref, sems):
    groups = all_ref.shape[0] // CAPR
    block_of = lax.broadcasted_iota(jnp.int32, (CAPR, LANES), 1) // CAPR
    filled = jnp.zeros((CAPR, LANES), jnp.float32)
    for g in range(0, groups, 2):
        got = []
        for r in range(PACK):
            at = ((g // lots * PACK + r) * lots + g % lots) * ROWS
            got.append(got_ref[at:at + 2 * ROWS, :].astype(jnp.float32))
        both = []
        for odd in range(2):
            m = [x[odd * ROWS:odd * ROWS + CAPR] for x in got]
            rest = swap_blocks(jnp.concatenate([x[odd * ROWS + CAPR:(odd + 1) * ROWS] for x in got], axis=0))
            filled = filled + (m[0] > 0).astype(jnp.float32)
            tiles = []
            for t in range(PACK + 1):
                tile = rest
                if t > 0:
                    tile = jnp.where(block_of < t - 1, m[t - 1], tile)
                if t < PACK:
                    tile = jnp.where(block_of >= t, m[t], tile)
                tiles.append(tile)
            both.append(jnp.concatenate(tiles, axis=1))
        all_ref[g * CAPR:(g + 2) * CAPR, :] = jnp.concatenate(both, axis=0).astype(jnp.bfloat16)
    series = all_ref[...]
    sums = dot(jnp.ones((8, series.shape[0]), jnp.bfloat16), series)
    count = jnp.sum(filled, axis=0, keepdims=True)[:, :1]
    left = count / sums.T[:, :1]
    right = 1.0 / sums[:1]
    outs = []
    total = series.shape[1]
    for t in range(0, total, TALL):
        rows = pl.ds(t, TALL)
        block = dot(all_ref[:, t:t + TALL], all_ref[:, t:], TN) * left[t:t + TALL] * right[:, t:]
        hold_ref[rows, t:] = block
        for u in range(t + TALL, total, TALL):
            hold_ref[u:u + TALL, t:t + TALL] = block[:, u - t:u - t + TALL].T
        outs.append(pltpu.make_async_copy(hold_ref.at[rows], out_ref.at[0, rows], sems.at[t // TALL]))
        outs[-1].start()
    for copy in outs:
        copy.wait()


def correlate(got, total, lots=8):
    slots = got.shape[0] * LANES // total
    return pl.pallas_call(
        functools.partial(gram_kernel, lots),
        out_shape=jax.ShapeDtypeStruct((1, total, total), jnp.float32),
        in_specs=[pl.BlockSpec(memory_space=pltpu.VMEM)],
        out_specs=pl.BlockSpec(memory_space=pl.ANY),
        scratch_shapes=[
            pltpu.VMEM((slots, total), jnp.bfloat16),
            pltpu.VMEM((total, total), jnp.float32),
            pltpu.SemaphoreType.DMA((total // TALL,)),
        ],
        compiler_params=pltpu.CompilerParams(vmem_limit_bytes=48 * 2**20),
        name="correlate",
    )(got)


def body(intensity, labels):
    readers, blks = lax.axis_size("reader"), lax.axis_size("blk")
    outgoing = pick(intensity, labels, readers, blks)
    got = lax.all_to_all(outgoing, ROUTE, split_axis=0, concat_axis=0, tiled=True)
    return correlate(got, intensity.shape[0] * readers, lax.axis_size("pixel"))


def solution(mesh):
    placed = (P("reader", ("pixel", "blk")), P(("pixel", "blk"), None))
    return jax.shard_map(
        body,
        mesh=mesh,
        in_specs=placed,
        out_specs=P(AXES, None, None),
        check_vma=False,
    )
```

```python
import functools

import jax
import jax.numpy as jnp
from jax import lax
from jax.experimental import pallas as pl
from jax.experimental.pallas import tpu as pltpu
from jax.sharding import PartitionSpec as P

CYCLES = 256
CAPR = 32
AXES = ("reader", "pixel", "blk")
ROUTE = ("blk", "pixel", "reader")
LANES = 128
WIDE = 256
PACK = LANES // CAPR
SHORT = CAPR // PACK
ROWS = CAPR + SHORT
PARTS = 4
CHUNKS = 8
GROUP = 8
TALL = 128
NN = (((1,), (0,)), ((), ()))
NT = (((1,), (1,)), ((), ()))
TN = (((0,), (0,)), ((), ()))


def dot(a, b, dims=NN):
    return lax.dot_general(a, b, dims, preferred_element_type=jnp.float32)


def swap_blocks(tile):
    height = tile.shape[0] // PACK
    block_of = lax.broadcasted_iota(jnp.int32, (height, LANES), 1) // CAPR
    turned = []
    for a in range(PACK):
        part = tile[a * height:(a + 1) * height]
        turned.append(pltpu.roll(part, CAPR * a, 1) if a else part)
    out = []
    for b in range(PACK):
        merged = turned[(0 - b) % PACK]
        for j in range(1, PACK):
            merged = jnp.where(block_of == j, turned[(j - b) % PACK], merged)
        out.append(pltpu.roll(merged, LANES - CAPR * b, 1) if b else merged)
    return jnp.concatenate(out, axis=0)


def pick_kernel(readers, blks, lab_hbm, x_ref, out_ref, lab_ref, frames_ref, place_ref, table_ref, main_ref, rest_ref,
                send_ref, scalars, sems, small_sems, out_sems):
    pixels = x_ref.shape[1]
    part = pixels // PARTS
    turn = lax.axis_index("reader")
    lab_copy = pltpu.make_async_copy(lab_hbm, lab_ref, small_sems.at[0])
    lab_copy.start()
    copies = []
    for b in range(PACK):
        to = pl.multiple_of(((b + turn) % PACK) * CAPR, CAPR)
        copies.append(pltpu.make_async_copy(x_ref.at[pl.ds(b * CAPR, CAPR)], frames_ref.at[pl.ds(to, CAPR)], sems.at[b]))
    copies.append(pltpu.make_async_copy(x_ref.at[pl.ds(LANES, CAPR)], frames_ref.at[pl.ds(LANES, CAPR)], sems.at[PACK]))

    row = lax.broadcasted_iota(jnp.int32, (WIDE, WIDE), 0)
    col = lax.broadcasted_iota(jnp.int32, (WIDE, WIDE), 1)
    lots = CYCLES // (readers * blks)
    line = row // readers
    name = (row % readers) * (CYCLES // readers) + (line % lots) * blks + line // lots
    upper = (row < col).astype(jnp.bfloat16)
    lower = (col < row).astype(jnp.bfloat16)
    ones = jnp.ones((WIDE, LANES), jnp.bfloat16)
    blocks = part // WIDE
    lab_copy.wait()
    for copy in copies:
        copy.start()
    earliers = []
    for begin in range(0, pixels // WIDE, GROUP):
        member = jnp.concatenate(
            [(lab_ref[:, i * WIDE:(i + 1) * WIDE] == name).astype(jnp.bfloat16) for i in range(begin, begin + GROUP)], axis=0)
        earliers.append(dot(member, upper))
    earlier = jnp.concatenate(earliers, axis=0)
    done = jnp.zeros((CYCLES, LANES), jnp.float32)
    for h in range(PARTS):
        count = []
        for i in range(h * blocks, (h + 1) * blocks):
            last = earlier[i * CYCLES:(i + 1) * CYCLES, WIDE - 1:] + (lab_ref[:, (i + 1) * WIDE - 1:(i + 1) * WIDE] == name[:, :1]).astype(jnp.float32)
            count.append(jnp.broadcast_to(last, (CYCLES, LANES)))
        total = functools.reduce(lambda a, b: a + b, count)
        base = dot(lower, total.astype(jnp.bfloat16))
        table_ref[2 * h:2 * h + 1, :] = (base - done + CAPR).T[:1].astype(jnp.int32)
        done = done + total
        table_ref[2 * h + 1:2 * h + 2, :] = done.T[:1].astype(jnp.int32)
        for i in range(blocks):
            at = h * part + i * WIDE
            from_row = (h * blocks + i) * CYCLES
            spot = earlier[from_row:from_row + CYCLES] + jnp.concatenate([base, base], axis=1)
            place_ref[:, at:at + WIDE] = jnp.sum(
                jnp.where(lab_ref[:, at:at + WIDE] == name, spot, 0.0), axis=0, keepdims=True)
            base = base + count[i]
    table_copy = pltpu.make_async_copy(table_ref, scalars, small_sems.at[1])
    table_copy.start()

    for copy in copies:
        copy.wait()
    for b in range(1, PACK):
        frames_ref[LANES + b * CAPR:LANES + (b + 1) * CAPR, :] = frames_ref[LANES:LANES + CAPR, :]
    spot = lax.broadcasted_iota(jnp.int32, (part, part), 0).astype(jnp.float32)
    block_of = lax.broadcasted_iota(jnp.int32, (CAPR + part, LANES), 1) // CAPR
    for h in range(PARTS):
        chosen = (spot == place_ref[:, h * part:(h + 1) * part]).astype(jnp.bfloat16)
        ordered = dot(chosen, frames_ref[:, h * part:(h + 1) * part], NT)
        main_ref[h, CAPR:CAPR + part, :] = ordered[:, :LANES]
        tail = jnp.concatenate([jnp.zeros((CAPR, LANES), jnp.float32), ordered[:, LANES:]], axis=0)
        folded = tail
        for q in range(1, PACK):
            shifted = jnp.concatenate([tail[q * SHORT:], tail[:q * SHORT]], axis=0)
            folded = jnp.where(block_of == q, shifted, folded)
        rest_ref[h, :CAPR + part, :] = folded

    table_copy.wait()
    slot = lax.broadcasted_iota(jnp.int32, (CAPR, LANES), 0)
    slot_rest = lax.broadcasted_iota(jnp.int32, (SHORT, LANES), 0) + SHORT * block_of[:SHORT]

    def spread(pair, carry):
        parts = []
        for odd in range(2):
            cycle = pair * 2 + odd
            main = jnp.zeros((CAPR, LANES), jnp.float32)
            rest = jnp.zeros((SHORT, LANES), jnp.float32)
            for h in reversed(range(PARTS)):
                at = scalars[2 * h, cycle]
                end = scalars[2 * h + 1, cycle]
                main = jnp.where(slot < end, main_ref[h, pl.ds(at, CAPR), :], main)
                rest = jnp.where(slot_rest < end, rest_ref[h, pl.ds(at, SHORT), :], rest)
            parts += [main, rest]
        to = pl.multiple_of(pair * (2 * ROWS), 2 * ROWS)
        send_ref[pl.ds(to, 2 * ROWS), :] = jnp.concatenate(parts, axis=0).astype(jnp.bfloat16)
        return carry

    pairs = CYCLES // 2 // CHUNKS
    outs = []
    for c in range(CHUNKS):
        lax.fori_loop(c * pairs, (c + 1) * pairs, spread, 0, unroll=16)
        rows = pl.ds(c * pairs * 2 * ROWS, pairs * 2 * ROWS)
        outs.append(pltpu.make_async_copy(send_ref.at[rows], out_ref.at[rows], out_sems.at[c]))
        outs[-1].start()
    for copy in outs:
        copy.wait()


def pick(intensity, labels, readers=4, blks=8):
    pixels = intensity.shape[1]
    part = pixels // PARTS
    return pl.pallas_call(
        functools.partial(pick_kernel, readers, blks),
        in_specs=[
            pl.BlockSpec(memory_space=pl.ANY),
            pl.BlockSpec(memory_space=pl.ANY),
        ],
        out_specs=pl.BlockSpec(memory_space=pl.ANY),
        out_shape=jax.ShapeDtypeStruct((CYCLES * ROWS, LANES), jnp.bfloat16),
        scratch_shapes=[
            pltpu.VMEM((1, pixels), jnp.int32),
            pltpu.VMEM((2 * LANES, pixels), jnp.bfloat16),
            pltpu.VMEM((1, pixels), jnp.float32),
            pltpu.VMEM((2 * PARTS, CYCLES), jnp.int32),
            pltpu.VMEM((PARTS, part + 2 * CAPR, LANES), jnp.float32),
            pltpu.VMEM((PARTS, part + 2 * CAPR, LANES), jnp.float32),
            pltpu.VMEM((CYCLES * ROWS, LANES), jnp.bfloat16),
            pltpu.SMEM((2 * PARTS, CYCLES), jnp.int32),
            pltpu.SemaphoreType.DMA((2 * PACK,)),
            pltpu.SemaphoreType.DMA((2,)),
            pltpu.SemaphoreType.DMA((CHUNKS,)),
        ],
        compiler_params=pltpu.CompilerParams(vmem_limit_bytes=60 * 2**20),
        name="pick_pixels",
    )(labels.reshape(1, pixels), intensity)


def gram_kernel(got_ref, out_ref, all_ref, hold_ref, sems):
    groups = all_ref.shape[0] // CAPR
    block_of = lax.broadcasted_iota(jnp.int32, (CAPR, LANES), 1) // CAPR
    filled = jnp.zeros((CAPR, LANES), jnp.float32)
    for g in range(0, groups, 2):
        got = [got_ref[(g + odd) * PACK * ROWS:(g + odd + 1) * PACK * ROWS, :].astype(jnp.float32) for odd in range(2)]
        both = []
        for odd in range(2):
            m = [got[odd][r * ROWS:r * ROWS + CAPR] for r in range(PACK)]
            rest = swap_blocks(jnp.concatenate([got[odd][r * ROWS + CAPR:(r + 1) * ROWS] for r in range(PACK)], axis=0))
            filled = filled + (m[0] > 0).astype(jnp.float32)
            tiles = []
            for t in range(PACK + 1):
                tile = rest
                if t > 0:
                    tile = jnp.where(block_of < t - 1, m[t - 1], tile)
                if t < PACK:
                    tile = jnp.where(block_of >= t, m[t], tile)
                tiles.append(tile)
            both.append(jnp.concatenate(tiles, axis=1))
        all_ref[g * CAPR:(g + 2) * CAPR, :] = jnp.concatenate(both, axis=0).astype(jnp.bfloat16)
    series = all_ref[...]
    sums = dot(jnp.ones((8, series.shape[0]), jnp.bfloat16), series)
    count = jnp.sum(filled, axis=0, keepdims=True)[:, :1]
    left = count / sums.T[:, :1]
    right = 1.0 / sums[:1]
    outs = []
    total = series.shape[1]
    for t in range(0, total, TALL):
        rows = pl.ds(t, TALL)
        block = dot(all_ref[:, t:t + TALL], all_ref[:, t:], TN) * left[t:t + TALL] * right[:, t:]
        hold_ref[rows, t:] = block
        for u in range(t + TALL, total, TALL):
            hold_ref[u:u + TALL, t:t + TALL] = block[:, u - t:u - t + TALL].T
        outs.append(pltpu.make_async_copy(hold_ref.at[rows], out_ref.at[0, rows], sems.at[t // TALL]))
        outs[-1].start()
    for copy in outs:
        copy.wait()


def correlate(got, total):
    slots = got.shape[0] * LANES // total
    return pl.pallas_call(
        gram_kernel,
        out_shape=jax.ShapeDtypeStruct((1, total, total), jnp.float32),
        in_specs=[pl.BlockSpec(memory_space=pltpu.VMEM)],
        out_specs=pl.BlockSpec(memory_space=pl.ANY),
        scratch_shapes=[
            pltpu.VMEM((slots, total), jnp.bfloat16),
            pltpu.VMEM((total, total), jnp.float32),
            pltpu.SemaphoreType.DMA((total // TALL,)),
        ],
        compiler_params=pltpu.CompilerParams(vmem_limit_bytes=48 * 2**20),
        name="correlate",
    )(got)


def body(intensity, labels):
    readers, blks = lax.axis_size("reader"), lax.axis_size("blk")
    outgoing = pick(intensity, labels, readers, blks)
    got = lax.all_to_all(outgoing, ROUTE, split_axis=0, concat_axis=0, tiled=True)
    return correlate(got, intensity.shape[0] * readers)


def solution(mesh):
    placed = (P("reader", ("pixel", "blk")), P(("pixel", "blk"), None))
    return jax.shard_map(
        body,
        mesh=mesh,
        in_specs=placed,
        out_specs=P(AXES, None, None),
        check_vma=False,
    )
```
